256 devices in a mesh: dp: 16 (over z, core), expert: 16 (over y, x).
Axes of the slice: x: 4, y: 4, z: 8, core: 2. Of those that a mesh axis runs over, the one named last changes fastest.
Arguments:
- tokens: bfloat16 [32768, 2048], P(('dp', 'expert')), may hold values from -6 to 6
- grad_out: bfloat16 [32768, 2048], P(('dp', 'expert')), may hold values from -6 to 6
- routes: int32 [32768, 4], P(('dp', 'expert')), may hold values from 0 to 15, all different within a row; in each aligned block of 128 rows (0 to 127, 128 to 255, ...) at most 40 rows name the same one
- combine: float32 [32768, 4], P(('dp', 'expert')), may hold values from 0.1 to 1
- w_gate: bfloat16 [16, 2048, 704], P('expert'), may hold values from -0.125 to 0.125
- w_up: bfloat16 [16, 2048, 704], P('expert'), may hold values from -0.125 to 0.125
- w_down: bfloat16 [16, 2048, 704], P('expert'), may hold values from -0.21875 to 0.21875
Outputs:
- grad_tokens: bfloat16 [32768, 2048], P(('dp', 'expert'))
- grad_gate: float32 [16, 2048, 704], P('expert', 'dp')
- grad_upper: float32 [16, 2048, 704], P('expert', 'dp')
- grad_down: float32 [16, 2048, 704], P('expert', 'dp')
The draws below stay inside these ranges and needn't reach their ends.
Inputs may be any that keep to these rules, and one draw needn't show every extreme that they name: `routes`: within the rows of one device (aligned blocks of 128 tokens), no expert is named more than 40 times, a bound that some block reaches; a token's 4 experts differ.
All inputs are finite; a program needn't handle non-finite values.
Results may differ from the reference program's by a relative error of at most 0.023.
Values may be sent and summed in bfloat16 or wider, within the bound.
A program may use at most 320 MiB of HBM per device.

```python
import math
import jax
import jax.numpy as jnp
import numpy as np
from jax import lax

D = 2048
HID = 704
TOPK = 4
TOK_DEV = 128
EXPERTS = 16
TOKENS = 32768
CAP = 40


def shard_levels(own_key, shape, shards, low, top_value):
    factor_of, own = 1.0, jax.random.fold_in(own_key, 6)
    for dim, blocks in shards:
        draws = jnp.exp(jax.random.uniform(jax.random.fold_in(own, dim), (blocks,), jnp.float32, low / len(shards), top_value / len(shards)))
        factor_of = factor_of * jnp.repeat(draws, shape[dim] // blocks).reshape([-1 if axis == dim else 1 for axis in range(len(shape))])
    return factor_of


def deal_out(own_key, own, number, rows, amount, top, reach, skew):
    sequence = jax.random.permutation(own_key, amount)
    packed, usual = load_shares(amount, rows * top, reach, skew, True), load_shares(amount, rows * top, reach, skew, False)
    places = jnp.arange(amount)

    def named(lengths, rotation):
        used = int((lengths > 0).sum())
        fixed = max(1, used // 4)
        moved = fixed + (places - fixed + rotation * (used - fixed)) % max(1, amount - fixed)
        return jnp.zeros((amount,), jnp.int32).at[sequence[jnp.where(places < fixed, places, moved)]].set(jnp.asarray(lengths, jnp.int32))

    lengths = jnp.where(number % 4 == 0, named(packed, number // 4), named(usual, number - number // 4 - 1))
    mixed = jax.random.permutation(jax.random.fold_in(own, 3), amount)
    donor, sink = mixed[0:amount // 2 * 2:2], mixed[1:amount // 2 * 2:2]
    slack = jnp.minimum(lengths[donor] - 1, reach - lengths[sink]) // 2
    slack = jnp.where((donor == sequence[0]) | (sink == sequence[0]) | (lengths[sink] == 0), 0, jnp.maximum(slack, 0))
    moved = jax.random.randint(jax.random.fold_in(own, 4), (amount // 2,), 0, 1 << 20) % (slack + 1)
    lengths = lengths.at[donor].add(-moved).at[sink].add(moved)
    members = jnp.searchsorted(jnp.cumsum(lengths), jnp.arange(rows * top), side="right").astype(jnp.int32)
    table = members.reshape(top, rows).T
    table = table[jax.random.permutation(jax.random.fold_in(own, 1), rows)]
    rotation = jax.random.randint(jax.random.fold_in(own, 2), (rows, 1), 0, top)
    return jnp.take_along_axis(table, (jnp.arange(top)[None, :] + rotation) % top, axis=1)


def load_shares(number_of, total, bound, lean, full):
    weights = [(1 << 20) // math.isqrt(rank ** lean) + 1 for rank in range(1, number_of + 1)]
    largest = bound if full else min(bound, max(-(-total // number_of), total * weights[0] // sum(weights)))
    least = 1 if total - largest >= number_of - 1 else 0
    counts, rest = [largest] + [least] * (number_of - 1), total - largest - least * (number_of - 1)
    while rest > 0:
        free = [i for i in range(1, number_of) if counts[i] < largest] or [i for i in range(1, number_of) if counts[i] < bound]
        mass, budget = sum([weights[i] for i in free]), rest
        for i in free:
            addition = min(bound - counts[i], max(1, budget * weights[i] // mass), rest)
            counts[i] = counts[i] + addition
            rest = rest - addition
    return np.array(counts)


def gaussian(key, shape, deviation, most, split=(), held_as=jnp.bfloat16):
    entries = jax.random.normal(key, shape, jnp.float32) * deviation
    if len(split) > 0:
        entries = shard_levels(key, shape, split, -0.22, 0.18) * entries
    return jnp.clip(entries, min=-most, max=most).astype(held_as)


def setup_inputs(seed: int = 0) -> dict:
    key_list = jax.random.split(jax.random.key(seed), 8)
    tokens = gaussian(key_list[0], (TOKENS, D), 1.0, 6.0, ((0, 256),))
    grad_out = gaussian(key_list[1], (TOKENS, D), 1.0, 6.0, ((0, 256),))
    routes_keys = jax.random.split(jax.random.fold_in(key_list[2], 1), TOKENS // TOK_DEV)
    routes_turns = jax.random.permutation(jax.random.fold_in(key_list[2], 3), TOKENS // TOK_DEV)
    routes = jax.vmap(lambda own, number: deal_out(jax.random.fold_in(key_list[2], 2), own, number, TOK_DEV, EXPERTS, TOPK, CAP, 1))(routes_keys, routes_turns).reshape((TOKENS, TOPK))
    combine = jnp.clip(0.1 + 0.9 * jax.random.uniform(key_list[3], (TOKENS, TOPK), jnp.float32) ** shard_levels(key_list[3], (TOKENS, TOPK), ((0, 256),), -0.2, 0.2), 0.1, 1.0)
    w_gate = gaussian(key_list[4], (EXPERTS, D, HID), D ** -0.5, 0.125, ((0, 16),))
    w_up = gaussian(key_list[5], (EXPERTS, D, HID), D ** -0.5, 0.125, ((0, 16),))
    w_down = gaussian(key_list[6], (EXPERTS, D, HID), HID ** -0.5, 0.21875, ((0, 16),))
    return {"tokens": tokens, "grad_out": grad_out, "routes": routes, "combine": combine, "w_gate": w_gate, "w_up": w_up, "w_down": w_down}


def expert_terms(rows_in, rows_cot, wg, wu, wd):
    gate = jnp.dot(rows_in, wg, preferred_element_type=jnp.float32)
    upper = jnp.dot(rows_in, wu, preferred_element_type=jnp.float32)
    sigma = jax.nn.sigmoid(gate)
    active = gate * sigma
    hidden = (active * upper).astype(jnp.bfloat16)
    grad_hidden = jnp.dot(rows_cot, wd, preferred_element_type=jnp.float32)
    grad_g = (grad_hidden * upper * sigma * (1.0 + gate * (1.0 - sigma))).astype(jnp.bfloat16)
    grad_u = (grad_hidden * active).astype(jnp.bfloat16)
    back = lax.dot_general(grad_g, wg, (((1,), (1,)), ((), ())), preferred_element_type=jnp.float32)
    back = back + lax.dot_general(grad_u, wu, (((1,), (1,)), ((), ())), preferred_element_type=jnp.float32)
    return hidden, grad_g, grad_u, back.astype(jnp.bfloat16)


def reference(tokens, grad_out, routes, combine, w_gate, w_up, w_down):
    blocks = TOKENS // TOK_DEV
    width = TOK_DEV * TOPK
    flat_e = routes.reshape(blocks, width).astype(jnp.int32)
    onehot = (flat_e[:, :, None] == jnp.arange(EXPERTS, dtype=jnp.int32)[None, None, :]).astype(jnp.int32)
    before = jnp.cumsum(onehot, axis=1) - onehot
    slot = jnp.sum(before * onehot, axis=2).astype(jnp.int32)
    position = (jnp.arange(blocks, dtype=jnp.int32)[:, None] * CAP + slot).astype(jnp.int32)
    flat_id = jnp.arange(TOKENS * TOPK, dtype=jnp.int32).reshape(blocks, width)
    buffer_rows = blocks * CAP
    weights_flat = combine.reshape(-1)

    def per_expert(carry, expert_id):
        target = jnp.where(flat_e == expert_id, position, buffer_rows).reshape(-1).astype(jnp.int32)
        source = jnp.zeros((buffer_rows + 1,), jnp.int32).at[target].set(flat_id.reshape(-1) + 1)[:buffer_rows]
        live = source > 0
        index = jnp.maximum(source - 1, 0).astype(jnp.int32)
        token_id = (index // TOPK).astype(jnp.int32)
        rows_in = jnp.where(live[:, None], tokens[token_id], jnp.zeros((), jnp.bfloat16))
        cot = weights_flat[index][:, None] * grad_out[token_id].astype(jnp.float32)
        rows_cot = jnp.where(live[:, None], cot, 0.0).astype(jnp.bfloat16)
        hidden, grad_g, grad_u, back = expert_terms(rows_in, rows_cot, w_gate[expert_id], w_up[expert_id], w_down[expert_id])
        dims = (((0,), (0,)), ((), ()))
        g_gate = lax.dot_general(rows_in, grad_g, dims, preferred_element_type=jnp.float32)
        g_upper = lax.dot_general(rows_in, grad_u, dims, preferred_element_type=jnp.float32)
        g_down = lax.dot_general(rows_cot, hidden, dims, preferred_element_type=jnp.float32)
        carry = carry.at[token_id].add(jnp.where(live[:, None], back.astype(jnp.float32), 0.0))
        return carry, (g_gate, g_upper, g_down)

    start = jnp.zeros((TOKENS, D), jnp.float32)
    total, grads = lax.scan(per_expert, start, jnp.arange(EXPERTS, dtype=jnp.int32))
    return total.astype(jnp.bfloat16), grads[0], grads[1], grads[2]
```

```python
import jax
import jax.numpy as jnp
from jax import lax
from jax.experimental import pallas as pl
from jax.experimental.pallas import tpu as pltpu
from jax.sharding import PartitionSpec as P

MESH = pl.DeviceIdType.MESH
BF = jnp.bfloat16
F32 = jnp.float32
TOK, WID, HID, CAP, NEXP = 128, 2048, 704, 40, 16
FB = 256
ROWS = 4 * CAP
ALL = 4 * ROWS
NN = (((1,), (0,)), ((), ()))
NT = (((1,), (1,)), ((), ()))
TN = (((0,), (0,)), ((), ()))


def dot(a, b, dims=NN):
    return lax.dot_general(a, b, dims, preferred_element_type=F32)


def kernel(
    tok_hbm, go_hbm, routes_ref, comb_ref, wg_hbm, wu_hbm, wd_hbm,
    out_tok, out_g, out_u, out_d,
    wg, wu, wd, meta, pmat, crow, tbuf, gbuf, tsend, ssend, xin, sin,
    gate, upper, gh, hidden, gg, gu, mine, csend, crecv, zsend, zrecv, brecv,
    wsem, lsem, ms, mr, ags, agr, a2s, a2r, cs, cr, zs, zr, bs, br, ps, pr,
):
    e = lax.axis_index("expert")
    d = lax.axis_index("dp")
    x, y, z, c = lax.rem(e, 4), e // 4, d // 2, lax.rem(d, 2)

    def along_y(r):
        return (d, lax.rem(y + r, 4) * 4 + x)

    def along_x(r):
        return (d, y * 4 + lax.rem(x + r, 4))

    def along_z(r):
        return (lax.rem(z + r + 8, 8) * 2 + c, e)

    other_core = (z * 2 + 1 - c, e)
    spread = (along_y, along_x)
    route = (along_x, along_y)

    def block(h, i):
        if h == 0:
            return lax.rem(z + 4 - i, 8)
        return lax.rem(z + 4 + i, 8) if i else z

    def remote(src, dst, ss, rs, dev):
        return pltpu.make_async_remote_copy(
            src_ref=src, dst_ref=dst, send_sem=ss, recv_sem=rs, device_id=dev, device_id_type=MESH
        )

    arrays = ((tok_hbm, tbuf), (go_hbm, gbuf))

    def load(a, h, i):
        cols = pl.ds(pl.multiple_of(block(h, i) * FB, FB), FB)
        return pltpu.make_async_copy(
            arrays[a][0].at[:, cols], arrays[a][1].at[h, i, pl.ds(0, TOK)], lsem.at[a, h, i]
        )

    for a in range(2):
        for i in range(4):
            for h in range(2):
                load(a, h, i).start()
    for m, (src, dst) in enumerate(((wg_hbm, wg), (wu_hbm, wu), (wd_hbm, wd))):
        for h in range(2):
            for i in range(4):
                rows = pl.ds(pl.multiple_of(block(h, i) * FB, FB), FB)
                pltpu.make_async_copy(
                    src.at[0, rows], dst.at[h, pl.ds(i * FB, FB)], wsem.at[m, h, i]
                ).start()

    def wait_weights(m):
        src, dst = ((wg_hbm, wg), (wu_hbm, wu), (wd_hbm, wd))[m]
        for h in range(2):
            for i in range(4):
                pltpu.make_async_copy(
                    src.at[0, pl.ds(0, FB)], dst.at[h, pl.ds(i * FB, FB)], wsem.at[m, h, i]
                ).wait()

    barrier = pltpu.get_barrier_semaphore()
    peers = [f(r) for f in (along_x, along_y) for r in (1, 2, 3)] + [along_z(1), along_z(-1), other_core]
    for dev in peers:
        pl.semaphore_signal(barrier, inc=1, device_id=dev, device_id_type=MESH)

    experts = lax.broadcasted_iota(jnp.int32, (TOK, 128), 1)
    taken = jnp.zeros((TOK, 128), F32)
    weight = jnp.zeros((TOK, 128), F32)
    for k in range(4):
        hit = routes_ref[:, k : k + 1] == experts
        taken = taken + jnp.where(hit, 1.0, 0.0)
        weight = weight + jnp.where(hit, comb_ref[:, k : k + 1], 0.0)
    earlier = (
        lax.broadcasted_iota(jnp.int32, (TOK, TOK), 0) > lax.broadcasted_iota(jnp.int32, (TOK, TOK), 1)
    ).astype(BF)
    slot = dot(earlier, taken.astype(BF))
    key = jnp.where(taken > 0.5, slot, -10000.0)
    for h in range(2):
        meta[h, 0, 0:NEXP, :] = key.T[0:NEXP]
        meta[h, 0, NEXP : 2 * NEXP, :] = weight.T[0:NEXP]

    pl.semaphore_wait(barrier, len(peers))

    for h in range(2):
        for r in (1, 2, 3):
            remote(meta.at[h, 0], meta.at[h, 4 - r], ms.at[h], mr.at[h], spread[h](r)).start()

    def gather_send(a, h, i):
        buf = arrays[a][1]
        for r in (1, 3, 2):
            remote(
                buf.at[h, i, pl.ds(0, TOK)],
                buf.at[h, i, pl.ds((4 - r) * TOK, TOK)],
                ags.at[a, h, i],
                agr.at[a, h, i],
                spread[h](r),
            ).start()

    def gather_all(a, h, i):
        part = arrays[a][1].at[h, i, pl.ds(TOK, 3 * TOK)]
        return remote(part, part, ags.at[a, h, i], agr.at[a, h, i], spread[h](1))

    for i in range(4):
        for h in range(2):
            load(0, h, i).wait()
            gather_send(0, h, i)

    for h in range(2):
        m = meta.at[h, pl.ds(1, 3)]
        remote(m, m, ms.at[h], mr.at[h], spread[h](1)).wait()
        for r in range(4):
            ex = route[h](r)[1]
            keys = jnp.concatenate([meta[h, s, pl.ds(ex, 1), :] + float(s * CAP) for s in range(4)], axis=1)
            wts = jnp.concatenate([meta[h, s, pl.ds(ex + NEXP, 1), :] for s in range(4)], axis=1)
            hit = lax.broadcasted_iota(jnp.int32, (ROWS, 4 * TOK), 0).astype(F32) == keys
            pmat[h, r * ROWS : (r + 1) * ROWS, :] = jnp.where(hit, 1.0, 0.0).astype(BF)
            crow[h, r * ROWS : (r + 1) * ROWS, :] = jnp.sum(jnp.where(hit, wts, 0.0), axis=1, keepdims=True)

    def second_send(a, h, i):
        snd, dst = ((tsend, xin), (ssend, sin))[a]
        for r in (2, 1, 3):
            remote(
                snd.at[h, i, pl.ds(r * ROWS, ROWS)],
                dst.at[h, i, pl.ds((4 - r) * ROWS, ROWS)],
                a2s.at[a, h, i],
                a2r.at[a, h, i],
                route[h](r),
            ).start()

    def second_all(a, h, i):
        snd, dst = ((tsend, xin), (ssend, sin))[a]
        return remote(
            snd.at[h, i, pl.ds(ROWS, 3 * ROWS)],
            dst.at[h, i, pl.ds(ROWS, 3 * ROWS)],
            a2s.at[a, h, i],
            a2r.at[a, h, i],
            route[h](1),
        )

    for i in range(4):
        for h in range(2):
            gather_all(0, h, i).wait_recv()
            rows = dot(pmat[h], tbuf[h, i]).astype(BF)
            xin[h, i, 0:ROWS, :] = rows[0:ROWS]
            tsend[h, i] = rows
            second_send(0, h, i)
            load(1, h, i).wait()
            gather_send(1, h, i)

    for i in range(4):
        for h in range(2):
            gather_all(1, h, i).wait_recv()
            rows = (dot(pmat[h], gbuf[h, i]) * crow[h]).astype(BF)
            sin[h, i, 0:ROWS, :] = rows[0:ROWS]
            ssend[h, i] = rows
            second_send(1, h, i)

    wait_weights(0)
    wait_weights(1)

    def project(src, w, h, rows):
        total = dot(src[h, 0, rows, :], w[h, 0:FB, :])
        for i in range(1, 4):
            total = total + dot(src[h, i, rows, :], w[h, i * FB : (i + 1) * FB, :])
        return total

    def add_other(acc, val, r):
        for s in range(4):
            at = pl.ds(pl.multiple_of(s * ROWS + r * CAP, 8), CAP)
            acc[at, :] = acc[at, :] + val[s * CAP : (s + 1) * CAP]

    def other_order(acc, r):
        return jnp.concatenate(
            [acc[pl.ds(pl.multiple_of(s * ROWS + r * CAP, 8), CAP), :] for s in range(4)], axis=0
        )

    def tile(r):
        return pl.ds(pl.multiple_of(r * ROWS, ROWS), ROWS)

    for i in range(4):
        second_all(0, 0, i).wait_recv()

    @pl.loop(0, 4)
    def _(r):
        gate[tile(r), :] = project(xin, wg, 0, tile(r))
        upper[tile(r), :] = project(xin, wu, 0, tile(r))

    for i in range(4):
        second_all(0, 1, i).wait_recv()

    @pl.loop(0, 4)
    def _(r):
        add_other(gate, project(xin, wg, 1, tile(r)), r)
        add_other(upper, project(xin, wu, 1, tile(r)), r)

    @pl.loop(0, 4)
    def _(r):
        g, u = gate[tile(r), :], upper[tile(r), :]
        s = jax.nn.sigmoid(g)
        active = g * s
        hid = active * u
        hidden[0, tile(r), :] = hid.astype(BF)
        gh[tile(r), :] = hid
        gate[tile(r), :] = u * s * (1.0 + g * (1.0 - s))
        upper[tile(r), :] = active

    @pl.loop(0, 4)
    def _(r):
        hidden[1, tile(r), :] = other_order(gh, r).astype(BF)

    outs = (out_d, out_g, out_u)

    def partial(m, h, i, rows_ref, factor):
        val = dot(rows_ref[h, i], factor[h], TN)
        low, high = val[0:TOK], val[TOK : 2 * TOK]
        own = jnp.where(c == 0, low, high)
        if h == 1 and i == 0:
            outs[m][0] = own
        else:
            mine[m, h] = own
        csend[m, h] = jnp.where(c == 0, high, low).astype(BF)
        remote(csend.at[m, h], crecv.at[m, h, i], cs.at[m, h, i], cr.at[m, h, i], other_core).start()

    def swapped(m, h, i):
        remote(csend.at[m, h], crecv.at[m, h, i], cs.at[m, h, i], cr.at[m, h, i], other_core).wait()

    def zcopy(m, h, i, rows=pl.ds(0, TOK)):
        return remote(
            zsend.at[m, h, i % 2, rows],
            zrecv.at[m, h, i, rows],
            zs.at[m, h, i],
            zr.at[m, h, i],
            along_z(1 if h == 0 else -1),
        )

    halves = (pl.ds(0, 64), pl.ds(64, 64))

    def forward(m, i):
        if i == 0:
            swapped(m, 0, 0)
            val = (mine[m, 0] + crecv[m, 0, 0].astype(F32)).astype(BF)
            for h in range(2):
                zsend[m, h, 0, halves[h], :] = val[64 * h : 64 * h + 64]
                zcopy(m, h, 0, halves[h]).start()
            swapped(m, 1, 0)
            outs[m][0] = outs[m][0] + crecv[m, 1, 0].astype(F32)
            return
        for h in range(2):
            swapped(m, h, i)
            if i == 1:
                zcopy(m, h, 0, halves[h]).wait_recv()
                val = mine[m, h] + crecv[m, h, 1].astype(F32)
                got = zrecv[m, h, 0, halves[h], :].astype(F32)
                keep = val[64 * (1 - h) : 64 * (1 - h) + 64]
                zsend[m, h, 1, halves[h], :] = (val[64 * h : 64 * h + 64] + got).astype(BF)
                zsend[m, h, 1, halves[1 - h], :] = keep.astype(BF)
            else:
                zcopy(m, h, i - 1).wait_recv()
                if i == 2:
                    zcopy(m, h, 0, halves[h]).wait_send()
                else:
                    zcopy(m, h, i - 2).wait_send()
                val = mine[m, h] + crecv[m, h, i].astype(F32) + zrecv[m, h, i - 1].astype(F32)
                zsend[m, h, i % 2] = val.astype(BF)
            zcopy(m, h, i).start()

    def settle(m):
        for h in range(2):
            zcopy(m, h, 3).wait_recv()
            zcopy(m, h, 2).wait_send()
            zcopy(m, h, 3).wait_send()
        outs[m][0] = outs[m][0] + (zrecv[m, 0, 3].astype(F32) + zrecv[m, 1, 3].astype(F32))

    for i in range(4):
        for h in range(2):
            second_all(1, h, i).wait_recv()
            partial(0, h, i, sin, hidden)
        forward(0, i)

    wait_weights(2)

    @pl.loop(0, 4)
    def _(r):
        gh[tile(r), :] = project(sin, wd, 0, tile(r))

    @pl.loop(0, 4)
    def _(r):
        add_other(gh, project(sin, wd, 1, tile(r)), r)

    @pl.loop(0, 4)
    def _(r):
        v = gh[tile(r), :]
        a = v * gate[tile(r), :]
        b = v * upper[tile(r), :]
        gate[tile(r), :] = a
        upper[tile(r), :] = b
        gg[0, tile(r), :] = a.astype(BF)
        gu[0, tile(r), :] = b.astype(BF)

    @pl.loop(0, 4)
    def _(r):
        gg[1, tile(r), :] = other_order(gate, r).astype(BF)
        gu[1, tile(r), :] = other_order(upper, r).astype(BF)

    def back_copy(h, i, r):
        return remote(
            tsend.at[h, i, pl.ds(r * ROWS, ROWS)],
            brecv.at[h, i, pl.ds((4 - r) * ROWS, ROWS)],
            bs.at[h, i],
            br.at[h, i],
            route[h](r),
        )

    def back_all(h, i):
        return remote(
            tsend.at[h, i, pl.ds(ROWS, 3 * ROWS)],
            brecv.at[h, i, pl.ds(ROWS, 3 * ROWS)],
            bs.at[h, i],
            br.at[h, i],
            route[h](1),
        )

    def back(h, i):
        at = slice(i * FB, (i + 1) * FB)
        second_all(0, h, i).wait_send()
        val = (dot(gg[h], wg[h, at, :], NT) + dot(gu[h], wu[h, at, :], NT)).astype(BF)
        brecv[h, i, 0:ROWS, :] = val[0:ROWS]
        tsend[h, i] = val
        for r in (2, 1, 3):
            back_copy(h, i, r).start()

    def home_all(h, i):
        return remote(
            ssend.at[h, i, pl.ds(TOK, 3 * TOK)],
            tbuf.at[h, i, pl.ds(TOK, 3 * TOK)],
            ps.at[h, i],
            pr.at[h, i],
            spread[h](1),
        )

    def home(h, i):
        back_all(h, i).wait_recv()
        second_all(1, h, i).wait_send()
        gather_all(0, h, i).wait_send()
        val = dot(pmat[h], brecv[h, i], TN).astype(BF)
        tbuf[h, i, 0:TOK, :] = val[0:TOK]
        ssend[h, i, 0 : 4 * TOK, :] = val
        for s in (1, 3, 2):
            remote(
                ssend.at[h, i, pl.ds(s * TOK, TOK)],
                tbuf.at[h, i, pl.ds((4 - s) * TOK, TOK)],
                ps.at[h, i],
                pr.at[h, i],
                spread[h](s),
            ).start()

    def finish(h, i):
        home_all(h, i).wait_recv()
        total = tbuf[h, i, 0:TOK, :].astype(F32)
        for s in range(1, 4):
            total = total + tbuf[h, i, s * TOK : (s + 1) * TOK, :].astype(F32)
        cols = pl.ds(pl.multiple_of(block(h, i) * FB, FB), FB)
        out_tok[:, cols] = total.astype(BF)

    def partials(i):
        for h in range(2):
            partial(1, h, i, xin, gg)
            partial(2, h, i, xin, gu)

    def both(f, i):
        f(0, i)
        f(1, i)

    partials(0)
    both(back, 0)
    forward(1, 0)
    forward(2, 0)
    settle(0)
    for i in (1, 2, 3):
        both(back, i)
    partials(1)
    both(home, 0)
    both(home, 1)
    forward(1, 1)
    forward(2, 1)
    partials(2)
    both(home, 2)
    both(home, 3)
    both(finish, 0)
    forward(1, 2)
    forward(2, 2)
    partials(3)
    for i in (1, 2, 3):
        both(finish, i)
    forward(1, 3)
    forward(2, 3)
    settle(1)
    settle(2)

    for h in range(2):
        for i in range(4):
            gather_all(1, h, i).wait_send()
            back_all(h, i).wait_send()
            home_all(h, i).wait_send()


def local(tokens, grad_out, routes, combine, w_gate, w_up, w_down):
    vm = pl.BlockSpec(memory_space=pltpu.VMEM)
    hbm = pl.BlockSpec(memory_space=pl.ANY)
    grad = jax.ShapeDtypeStruct((1, TOK, HID), F32)
    sem = pltpu.SemaphoreType.DMA
    V = pltpu.VMEM
    return pl.pallas_call(
        kernel,
        name="experts",
        out_shape=(jax.ShapeDtypeStruct((TOK, WID), BF), grad, grad, grad),
        in_specs=[hbm, hbm, vm, vm, hbm, hbm, hbm],
        out_specs=(vm, vm, vm, vm),
        scratch_shapes=[
            V((2, 1024, HID), BF), V((2, 1024, HID), BF), V((2, 1024, HID), BF),
            V((2, 4, 2 * NEXP, 128), F32),
            V((2, ALL, 4 * TOK), BF),
            V((2, ALL, 1), F32),
            V((2, 4, 4 * TOK, FB), BF), V((2, 4, 4 * TOK, FB), BF),
            V((2, 4, ALL, FB), BF), V((2, 4, ALL, FB), BF),
            V((2, 4, ALL, FB), BF), V((2, 4, ALL, FB), BF),
            V((ALL, HID), F32), V((ALL, HID), F32), V((ALL, HID), F32),
            V((2, ALL, HID), BF), V((2, ALL, HID), BF), V((2, ALL, HID), BF),
            V((3, 2, TOK, HID), F32),
            V((3, 2, TOK, HID), BF),
            V((3, 2, 4, TOK, HID), BF),
            V((3, 2, 2, TOK, HID), BF),
            V((3, 2, 4, TOK, HID), BF),
            V((2, 4, ALL, FB), BF),
            sem((3, 2, 4)), sem((2, 2, 4)), sem((2,)), sem((2,)),
            sem((2, 2, 4)), sem((2, 2, 4)), sem((2, 2, 4)), sem((2, 2, 4)),
            sem((3, 2, 4)), sem((3, 2, 4)), sem((3, 2, 4)), sem((3, 2, 4)),
            sem((2, 4)), sem((2, 4)), sem((2, 4)), sem((2, 4)),
        ],
        compiler_params=pltpu.CompilerParams(
            collective_id=0, has_side_effects=True, vmem_limit_bytes=62 * 2**20
        ),
        cost_estimate=pl.CostEstimate(flops=15 * 10**9, bytes_accessed=12 * 10**6, transcendentals=450560),
    )(tokens, grad_out, routes, combine, w_gate, w_up, w_down)


def solution(mesh):
    rows = P(("dp", "expert"), None)
    weights = P("expert", None, None)
    grads = P("expert", "dp", None)
    return jax.shard_map(
        local,
        mesh=mesh,
        in_specs=(rows, rows, rows, rows, weights, weights, weights),
        out_specs=(rows, grads, grads, grads),
        check_vma=False,
    )
```

```python
import jax
import jax.numpy as jnp
from jax import lax
from jax.experimental import pallas as pl
from jax.experimental.pallas import tpu as pltpu
from jax.sharding import PartitionSpec as P

AHEAD = 3
LOOK, LAG, PASS = 6, 3, True
MESH = pl.DeviceIdType.MESH
BF = jnp.bfloat16
F32 = jnp.float32
TOK, WID, HID, CAP, NEXP = 128, 2048, 704, 40, 16
FB = 256
ROWS = 4 * CAP
ALL = 4 * ROWS
NN = (((1,), (0,)), ((), ()))
NT = (((1,), (1,)), ((), ()))
TN = (((0,), (0,)), ((), ()))


def dot(a, b, dims=NN):
    return lax.dot_general(a, b, dims, preferred_element_type=F32)


def kernel(
    tok_hbm, go_hbm, routes_ref, comb_ref, wg_hbm, wu_hbm, wd_hbm,
    out_tok, out_g, out_u, out_d,
    wg, wu, wd, meta, pmat, pback, crow, tbuf, gbuf, tsend, ssend, xin, sin,
    gate, upper, gh, hidden, ggt, gut, gg, gu, mine, last, csend, crecv, zsend, zrecv, brecv, home_rows,
    wsem, lsem, osem, ms, mr, ags, agr, a2s, a2r, cs, cr, zs, zr, bs, br, ps, pr,
):
    e = lax.axis_index("expert")
    d = lax.axis_index("dp")
    x, y, z, c = lax.rem(e, 4), e // 4, d // 2, lax.rem(d, 2)

    def along_y(r):
        return (d, lax.rem(y + r, 4) * 4 + x)

    def along_x(r):
        return (d, y * 4 + lax.rem(x + r, 4))

    def along_z(r):
        return (lax.rem(z + r + 8, 8) * 2 + c, e)

    other_core = (z * 2 + 1 - c, e)
    spread = (along_y, along_x)
    route = (along_x, along_y)

    def block(h, i):
        if h == 0:
            return lax.rem(z + 4 - i, 8)
        return lax.rem(z + 4 + i, 8) if i else z

    def remote(src, dst, ss, rs, dev):
        return pltpu.make_async_remote_copy(
            src_ref=src, dst_ref=dst, send_sem=ss, recv_sem=rs, device_id=dev, device_id_type=MESH
        )

    barrier = pltpu.get_barrier_semaphore()
    peers = [f(r) for f in (along_x, along_y) for r in (1, 2, 3)] + [along_z(1), along_z(-1), other_core]
    for dev in peers:
        pl.semaphore_signal(barrier, inc=1, device_id=dev, device_id_type=MESH)

    arrays = ((tok_hbm, tbuf), (go_hbm, gbuf))

    def load(a, h, i):
        cols = pl.ds(pl.multiple_of(block(h, i) * FB, FB), FB)
        return pltpu.make_async_copy(
            arrays[a][0].at[:, cols], arrays[a][1].at[h, i, pl.ds(0, TOK)], lsem.at[a, h, i]
        )

    for a in range(2):
        for i in range(4):
            for h in range(2):
                load(a, h, i).start()
    def wait_weights(m):
        src, dst = ((wg_hbm, wg), (wu_hbm, wu), (wd_hbm, wd))[m]
        for h in range(2):
            for i in range(4):
                pltpu.make_async_copy(src.at[0, :, pl.ds(0, FB)], dst.at[h, i], wsem.at[m, h, i]).wait()

    experts = lax.broadcasted_iota(jnp.int32, (NEXP, TOK), 0)
    taken = jnp.zeros((NEXP, TOK), F32)
    weight = jnp.zeros((NEXP, TOK), F32)
    for k in range(4):
        hit = routes_ref[k : k + 1, :] == experts
        taken = taken + jnp.where(hit, 1.0, 0.0)
        weight = weight + jnp.where(hit, comb_ref[k : k + 1, :], 0.0)
    earlier = (
        lax.broadcasted_iota(jnp.int32, (TOK, TOK), 0) < lax.broadcasted_iota(jnp.int32, (TOK, TOK), 1)
    ).astype(BF)
    key = jnp.where(taken > 0.5, dot(taken.astype(BF), earlier), -10000.0)
    for h in range(2):
        meta[h, 0, 0:NEXP, :] = key
        meta[h, 0, NEXP : 2 * NEXP, :] = weight

    pl.semaphore_wait(barrier, len(peers))

    for h in range(2):
        for r in (1, 2, 3):
            remote(meta.at[h, 0], meta.at[h, 4 - r], ms.at[h], mr.at[h], spread[h](r)).start()

    neighbour = (4 - 1, 1)

    def gather_own(a, h, i):
        load(a, h, i).wait()
        buf = arrays[a][1].at[h, i]
        for k, r in ((0, 1), (1, 3)) if PASS else ((0, 1), (1, 3), (2, 2)):
            remote(
                buf.at[pl.ds(0, TOK)],
                buf.at[pl.ds((4 - r) * TOK, TOK)],
                ags.at[a, h, i],
                agr.at[a, h, i, k],
                spread[h](r),
            ).start()

    def gather_pass(a, h, i):
        buf = arrays[a][1].at[h, i]
        for k, r in ((0, 1), (1, 3)):
            part = buf.at[pl.ds(neighbour[k] * TOK, TOK)]
            remote(part, part, ags.at[a, h, i], agr.at[a, h, i, k], spread[h](r)).wait_recv()
            if not PASS:
                continue
            remote(
                buf.at[pl.ds(neighbour[k] * TOK + k * (TOK // 2), TOK // 2)],
                buf.at[pl.ds(2 * TOK + k * (TOK // 2), TOK // 2)],
                ags.at[a, h, i],
                agr.at[a, h, i, 2],
                spread[h](r),
            ).start()

    def gather_far(a, h, i):
        part = arrays[a][1].at[h, i, pl.ds(2 * TOK, TOK)]
        remote(part, part, ags.at[a, h, i], agr.at[a, h, i, 2], spread[h](1)).wait_recv()

    def gather_all(a, h, i):
        part = arrays[a][1].at[h, i, pl.ds(TOK, 3 * TOK)]
        return remote(part, part, ags.at[a, h, i], agr.at[a, h, i, 0], spread[h](1))

    for n in range(LOOK):
        for h in range(2):
            gather_own(n // 4, h, n % 4)

    for m, (src, dst) in enumerate(((wg_hbm, wg), (wu_hbm, wu), (wd_hbm, wd))):
        for h in range(2):
            for i in range(4):
                cols = pl.ds(pl.multiple_of(block(h, i) * FB, FB), FB)
                pltpu.make_async_copy(src.at[0, :, cols], dst.at[h, i], wsem.at[m, h, i]).start()

    for h in range(2):
        m = meta.at[h, pl.ds(1, 3)]
        remote(m, m, ms.at[h], mr.at[h], spread[h](1)).wait()
        for r in range(4):
            ex = route[h](r)[1]
            keys = jnp.concatenate([meta[h, s, pl.ds(ex, 1), :] + float(s * CAP) for s in range(4)], axis=1)
            wts = jnp.concatenate([meta[h, s, pl.ds(ex + NEXP, 1), :] for s in range(4)], axis=1)
            hit = lax.broadcasted_iota(jnp.int32, (ROWS, 4 * TOK), 0).astype(F32) == keys
            pmat[h, r * ROWS : (r + 1) * ROWS, :] = jnp.where(hit, 1.0, 0.0).astype(BF)
            crow[h, r * ROWS : (r + 1) * ROWS, :] = jnp.sum(jnp.where(hit, wts, 0.0), axis=1, keepdims=True)

    def second_send(a, h, i):
        snd, dst = ((tsend, xin), (ssend, sin))[a]
        for r in (2, 1, 3):
            remote(
                snd.at[h, i, pl.ds(r * ROWS, ROWS)],
                dst.at[h, i, pl.ds((4 - r) * ROWS, ROWS)],
                a2s.at[a, h, i],
                a2r.at[a, h, i],
                route[h](r),
            ).start()

    def second_all(a, h, i):
        snd, dst = ((tsend, xin), (ssend, sin))[a]
        return remote(
            snd.at[h, i, pl.ds(ROWS, 3 * ROWS)],
            dst.at[h, i, pl.ds(ROWS, 3 * ROWS)],
            a2s.at[a, h, i],
            a2r.at[a, h, i],
            route[h](1),
        )

    def picked(a, h, i):
        gather_far(a, h, i)
        rows = dot(pmat[h], arrays[a][1][h, i])
        rows = (rows * crow[h] if a else rows).astype(BF)
        snd, dst = ((tsend, xin), (ssend, sin))[a]
        dst[h, i, 0:ROWS, :] = rows[0:ROWS]
        snd[h, i] = rows
        second_send(a, h, i)

    def exchange(n):
        for h in range(2):
            if n < 8 - AHEAD:
                gather_pass((n + AHEAD) // 4, h, (n + AHEAD) % 4)
            if n >= 4:
                gather_all(0, h, n - 4).wait_send()
        for h in range(2):
            picked(n // 4, h, n % 4)
        for h in range(2):
            if n >= LAG:
                second_all((n - LAG) // 4, h, (n - LAG) % 4).wait_send()
            if n < 8 - LOOK:
                gather_own((n + LOOK) // 4, h, (n + LOOK) % 4)

    def same_order(buf, i):
        val = buf[1, i].astype(F32)
        pieces = [val[p * ROWS + q * CAP : p * ROWS + (q + 1) * CAP] for q in range(4) for p in range(4)]
        buf[1, i] = jnp.concatenate(pieces, axis=0).astype(BF)

    def arrived(a, i):
        for h in range(2):
            second_all(a, h, i).wait_recv()
        same_order((xin, sin)[a], i)

    def big(r):
        return pl.ds(pl.multiple_of(r * 352, 352), 352)

    def tile(r):
        return pl.ds(pl.multiple_of(r * 176, 176), 176)

    def project(w, src, at, blocks):
        total = None
        for i in blocks:
            for h in range(2):
                term = dot(w[h, i, at, :], src[h, i], NT)
                total = term if total is None else total + term
        return total

    def gates(i):
        arrived(0, i)

        @pl.loop(0, 2)
        def _(r):
            for acc, w in ((gate, wg), (upper, wu)):
                val = project(w, xin, big(r), (i,))
                acc[big(r), :] = acc[big(r), :] + val if i else val

    def gates_end():
        @pl.loop(0, 4)
        def _(r):
            g, u = gate[tile(r), :], upper[tile(r), :]
            s = jax.nn.sigmoid(g)
            active = g * s
            hidden[tile(r), :] = (active * u).astype(BF)
            gate[tile(r), :] = u * s * (1.0 + g * (1.0 - s))
            upper[tile(r), :] = active

    outs = (out_d, out_g, out_u)

    def partial(m, h, i):
        val = dot((hidden, ggt, gut)[m][...], (sin if m == 0 else xin)[h, i])
        low, high = val[:, 0:TOK], val[:, TOK : 2 * TOK]
        own = jnp.where(c == 0, low, high)
        if h == 1 and i == 0:
            last[m] = own
        else:
            mine[m, h] = own
        csend[m, h] = jnp.where(c == 0, high, low).astype(BF)
        remote(csend.at[m, h], crecv.at[m, h, i], cs.at[m, h, i], cr.at[m, h, i], other_core).start()

    def swapped(m, h, i):
        remote(csend.at[m, h], crecv.at[m, h, i], cs.at[m, h, i], cr.at[m, h, i], other_core).wait()

    def zcopy(m, h, i, rows=pl.ds(0, HID)):
        return remote(
            zsend.at[m, h, i % 2, rows],
            zrecv.at[m, h, i, rows],
            zs.at[m, h, i],
            zr.at[m, h, i],
            along_z(1 if h == 0 else -1),
        )

    halves = (pl.ds(0, 352), pl.ds(352, 352))

    def forward(m, i):
        if i == 0:
            swapped(m, 0, 0)
            val = (mine[m, 0] + crecv[m, 0, 0].astype(F32)).astype(BF)
            for h in range(2):
                zsend[m, h, 0, halves[h], :] = val[352 * h : 352 * h + 352]
                zcopy(m, h, 0, halves[h]).start()
            return
        for h in range(2):
            swapped(m, h, i)
            if i == 1:
                zcopy(m, h, 0, halves[h]).wait_recv()
                val = mine[m, h] + crecv[m, h, 1].astype(F32)
                got = zrecv[m, h, 0, halves[h], :].astype(F32)
                keep = val[352 * (1 - h) : 352 * (1 - h) + 352]
                zsend[m, h, 1, halves[h], :] = (val[352 * h : 352 * h + 352] + got).astype(BF)
                zsend[m, h, 1, halves[1 - h], :] = keep.astype(BF)
            else:
                zcopy(m, h, i - 1).wait_recv()
                if i == 2:
                    zcopy(m, h, 0, halves[h]).wait_send()
                else:
                    zcopy(m, h, i - 2).wait_send()
                val = mine[m, h] + crecv[m, h, i].astype(F32) + zrecv[m, h, i - 1].astype(F32)
                zsend[m, h, i % 2] = val.astype(BF)
            zcopy(m, h, i).start()

    def settle(m):
        for h in range(2):
            zcopy(m, h, 3).wait_recv()
            zcopy(m, h, 2).wait_send()
            zcopy(m, h, 3).wait_send()
        near = last[m] + crecv[m, 1, 0].astype(F32)
        last[m] = near + (zrecv[m, 0, 3].astype(F32) + zrecv[m, 1, 3].astype(F32))
        pltpu.make_async_copy(last.at[m], outs[m].at[0], osem.at[m]).start()

    def back_copy(h, i, r):
        return remote(
            tsend.at[h, i, pl.ds(r * ROWS, ROWS)],
            brecv.at[h, i, pl.ds((4 - r) * ROWS, ROWS)],
            bs.at[h, i],
            br.at[h, i],
            route[h](r),
        )

    def back_all(h, i):
        return remote(
            tsend.at[h, i, pl.ds(ROWS, 3 * ROWS)],
            brecv.at[h, i, pl.ds(ROWS, 3 * ROWS)],
            bs.at[h, i],
            br.at[h, i],
            route[h](1),
        )

    def back(h, i):
        val = dot(gg[...], wg[h, i]) + dot(gu[...], wu[h, i])
        if h == 1:
            pieces = [val[p * ROWS + q * CAP : p * ROWS + (q + 1) * CAP] for q in range(4) for p in range(4)]
            val = jnp.concatenate(pieces, axis=0)
        val = val.astype(BF)
        brecv[h, i, 0:ROWS, :] = val[0:ROWS]
        tsend[h, i] = val
        for r in (2, 1, 3):
            back_copy(h, i, r).start()

    def home_all(h, i):
        return remote(
            ssend.at[h, i, pl.ds(TOK, 3 * TOK)],
            tbuf.at[h, i, pl.ds(TOK, 3 * TOK)],
            ps.at[h, i],
            pr.at[h, i],
            spread[h](1),
        )

    def home(h, i):
        back_all(h, i).wait_recv()
        if i >= 4 - LAG:
            second_all(1, h, i).wait_send()
        val = dot(pback[h], brecv[h, i]).astype(BF)
        tbuf[h, i, 0:TOK, :] = val[0:TOK]
        ssend[h, i, 0 : 4 * TOK, :] = val
        for s in (1, 3, 2):
            remote(
                ssend.at[h, i, pl.ds(s * TOK, TOK)],
                tbuf.at[h, i, pl.ds((4 - s) * TOK, TOK)],
                ps.at[h, i],
                pr.at[h, i],
                spread[h](s),
            ).start()

    def finish(h, i):
        home_all(h, i).wait_recv()
        total = tbuf[h, i, 0:TOK, :].astype(F32)
        for s in range(1, 4):
            total = total + tbuf[h, i, s * TOK : (s + 1) * TOK, :].astype(F32)
        cols = pl.ds(pl.multiple_of(block(h, i) * FB, FB), FB)
        home_rows[h, i] = total.astype(BF)
        pltpu.make_async_copy(home_rows.at[h, i], out_tok.at[:, cols], lsem.at[0, h, i]).start()

    def both(f, *args):
        f(0, *args)
        f(1, *args)

    def partials(m, i):
        partial(m, 0, i)
        partial(m, 1, i)

    def zero(m):
        partial(m, 1, 0)
        swapped(m, 1, 0)

    def down(i):
        arrived(1, i)
        partials(0, i) if i else partial(0, 0, 0)
        total = project(wd, sin, slice(None), (i,))
        gh[...] = total if i == 0 else gh[...] + total
        forward(0, i)

    for n in range(AHEAD):
        for h in range(2):
            gather_pass(0, h, n)
    exchange(0)
    exchange(1)
    exchange(2)
    wait_weights(0)
    wait_weights(1)
    gates(0)
    exchange(3)
    gates(1)
    exchange(4)
    gates(2)
    exchange(5)
    gates(3)
    gates_end()
    wait_weights(2)
    down(0)
    exchange(6)
    down(1)
    exchange(7)
    for h in range(2):
        pback[h] = pmat[h].T
    down(2)
    arrived(1, 3)
    partials(0, 3)

    @pl.loop(0, 2)
    def _(r):
        v = gh[big(r), :] + project(wd, sin, big(r), (3,))
        ggt[big(r), :] = (v * gate[big(r), :]).astype(BF)
        gut[big(r), :] = (v * upper[big(r), :]).astype(BF)

    partial(1, 0, 0)
    partial(2, 0, 0)
    forward(0, 3)
    gg[...] = ggt[...].T
    gu[...] = gut[...].T
    forward(1, 0)
    forward(2, 0)
    both(back, 0)
    partials(1, 1)
    both(back, 1)
    partials(2, 1)
    both(back, 2)
    forward(1, 1)
    forward(2, 1)
    both(back, 3)
    zero(0)
    settle(0)
    partials(1, 2)
    partials(2, 2)
    both(home, 0)
    both(home, 1)
    forward(1, 2)
    forward(2, 2)
    partials(1, 3)
    partials(2, 3)
    both(home, 2)
    both(home, 3)
    both(finish, 0)
    both(finish, 1)
    forward(1, 3)
    forward(2, 3)
    zero(1)
    zero(2)
    both(finish, 2)
    both(finish, 3)
    settle(1)
    settle(2)

    for h in range(2):
        for i in range(4):
            gather_all(1, h, i).wait_send()
            back_all(h, i).wait_send()
            home_all(h, i).wait_send()
            pltpu.make_async_copy(home_rows.at[h, i], out_tok.at[:, pl.ds(0, FB)], lsem.at[0, h, i]).wait()
    for m in range(3):
        pltpu.make_async_copy(last.at[m], outs[m].at[0], osem.at[m]).wait()


def deliver(*refs):
    for n in range(4):
        refs[4 + n][...] = refs[n][...]


def local(tokens, grad_out, routes, combine, w_gate, w_up, w_down):
    vm = pl.BlockSpec(memory_space=pltpu.VMEM)
    hbm = pl.BlockSpec(memory_space=pl.ANY)
    grad = jax.ShapeDtypeStruct((1, HID, TOK), F32)
    shapes = (jax.ShapeDtypeStruct((TOK, WID), BF), grad, grad, grad)
    sem = pltpu.SemaphoreType.DMA
    V = pltpu.VMEM
    parts = pl.pallas_call(
        kernel,
        name="experts",
        out_shape=shapes,
        in_specs=[hbm, hbm, vm, vm, hbm, hbm, hbm],
        out_specs=(hbm, hbm, hbm, hbm),
        scratch_shapes=[
            V((2, 4, HID, FB), BF), V((2, 4, HID, FB), BF), V((2, 4, HID, FB), BF),
            V((2, 4, 2 * NEXP, 128), F32),
            V((2, ALL, 4 * TOK), BF), V((2, 4 * TOK, ALL), BF),
            V((2, ALL, 1), F32),
            V((2, 4, 4 * TOK, FB), BF), V((2, 4, 4 * TOK, FB), BF),
            V((2, 4, ALL, FB), BF), V((2, 4, ALL, FB), BF),
            V((2, 4, ALL, FB), BF), V((2, 4, ALL, FB), BF),
            V((HID, ALL), F32), V((HID, ALL), F32), V((HID, ALL), F32),
            V((HID, ALL), BF), V((HID, ALL), BF), V((HID, ALL), BF),
            V((ALL, HID), BF), V((ALL, HID), BF),
            V((3, 2, HID, TOK), F32), V((3, HID, TOK), F32),
            V((3, 2, HID, TOK), BF),
            V((3, 2, 4, HID, TOK), BF),
            V((3, 2, 2, HID, TOK), BF),
            V((3, 2, 4, HID, TOK), BF),
            V((2, 4, ALL, FB), BF),
            V((2, 4, TOK, FB), BF),
            sem((3, 2, 4)), sem((2, 2, 4)), sem((3,)), sem((2,)), sem((2,)),
            sem((2, 2, 4)), sem((2, 2, 4, 3)), sem((2, 2, 4)), sem((2, 2, 4)),
            sem((3, 2, 4)), sem((3, 2, 4)), sem((3, 2, 4)), sem((3, 2, 4)),
            sem((2, 4)), sem((2, 4)), sem((2, 4)), sem((2, 4)),
        ],
        compiler_params=pltpu.CompilerParams(
            collective_id=0, has_side_effects=True, vmem_limit_bytes=62 * 2**20
        ),
        cost_estimate=pl.CostEstimate(flops=15 * 10**9, bytes_accessed=12 * 10**6, transcendentals=450560),
    )(tokens, grad_out, routes.T, combine.T, *[w.transpose(0, 2, 1) for w in (w_gate, w_up, w_down)])
    grad_tokens, *grads = pl.pallas_call(
        deliver,
        name="deliver",
        out_shape=shapes,
        in_specs=[vm] * 4,
        out_specs=(vm,) * 4,
    )(*parts)
    return (grad_tokens, *[g.transpose(0, 2, 1) for g in grads])


def solution(mesh):
    rows = P(("dp", "expert"), None)
    weights = P("expert", None, None)
    grads = P("expert", "dp", None)
    return jax.shard_map(
        local,
        mesh=mesh,
        in_specs=(rows, rows, rows, rows, weights, weights, weights),
        out_specs=(rows, grads, grads, grads),
        check_vma=False,
    )
```

```python
import jax
import jax.numpy as jnp
from jax import lax
from jax.experimental import pallas as pl
from jax.experimental.pallas import tpu as pltpu
from jax.sharding import PartitionSpec as P

AHEAD = 3
LOOK, LAG, PASS = 6, 3, True
MESH = pl.DeviceIdType.MESH
BF = jnp.bfloat16
F32 = jnp.float32
TOK, WID, HID, CAP, NEXP = 128, 2048, 704, 40, 16
FB = 256
ROWS = 4 * CAP
ALL = 4 * ROWS
NN = (((1,), (0,)), ((), ()))
NT = (((1,), (1,)), ((), ()))
TN = (((0,), (0,)), ((), ()))


def dot(a, b, dims=NN):
    return lax.dot_general(a, b, dims, preferred_element_type=F32)


def kernel(
    tok_hbm, go_hbm, routes_ref, comb_ref, wg_hbm, wu_hbm, wd_hbm,
    out_tok, out_g, out_u, out_d,
    wg, wu, wd, meta, pmat, pback, crow, tbuf, gbuf, tsend, ssend, xin, sin,
    gate, upper, gh, hidden, ggt, gut, gg, gu, mine, last, csend, crecv, zsend, zrecv, brecv, home_rows,
    wsem, lsem, osem, ms, mr, ags, agr, a2s, a2r, cs, cr, zs, zr, bs, br, ps, pr,
):
    e = lax.axis_index("expert")
    d = lax.axis_index("dp")
    x, y, z, c = lax.rem(e, 4), e // 4, d // 2, lax.rem(d, 2)

    def along_y(r):
        return (d, lax.rem(y + r, 4) * 4 + x)

    def along_x(r):
        return (d, y * 4 + lax.rem(x + r, 4))

    def along_z(r):
        return (lax.rem(z + r + 8, 8) * 2 + c, e)

    other_core = (z * 2 + 1 - c, e)
    spread = (along_y, along_x)
    route = (along_x, along_y)

    def block(h, i):
        if h == 0:
            return lax.rem(z + 4 - i, 8)
        return lax.rem(z + 4 + i, 8) if i else z

    def remote(src, dst, ss, rs, dev):
        return pltpu.make_async_remote_copy(
            src_ref=src, dst_ref=dst, send_sem=ss, recv_sem=rs, device_id=dev, device_id_type=MESH
        )

    barrier = pltpu.get_barrier_semaphore()
    peers = [f(r) for f in (along_x, along_y) for r in (1, 2, 3)] + [along_z(1), along_z(-1), other_core]
    for dev in peers:
        pl.semaphore_signal(barrier, inc=1, device_id=dev, device_id_type=MESH)

    arrays = ((tok_hbm, tbuf), (go_hbm, gbuf))

    def load(a, h, i):
        cols = pl.ds(pl.multiple_of(block(h, i) * FB, FB), FB)
        return pltpu.make_async_copy(
            arrays[a][0].at[:, cols], arrays[a][1].at[h, i, pl.ds(0, TOK)], lsem.at[a, h, i]
        )

    for a in range(2):
        for i in range(4):
            for h in range(2):
                load(a, h, i).start()
    def wait_weights(m):
        src, dst = ((wg_hbm, wg), (wu_hbm, wu), (wd_hbm, wd))[m]
        for h in range(2):
            for i in range(4):
                pltpu.make_async_copy(src.at[0, :, pl.ds(0, FB)], dst.at[h, i], wsem.at[m, h, i]).wait()

    experts = lax.broadcasted_iota(jnp.int32, (NEXP, TOK), 0)
    taken = jnp.zeros((NEXP, TOK), F32)
    weight = jnp.zeros((NEXP, TOK), F32)
    for k in range(4):
        hit = routes_ref[k : k + 1, :] == experts
        taken = taken + jnp.where(hit, 1.0, 0.0)
        weight = weight + jnp.where(hit, comb_ref[k : k + 1, :], 0.0)
    earlier = (
        lax.broadcasted_iota(jnp.int32, (TOK, TOK), 0) < lax.broadcasted_iota(jnp.int32, (TOK, TOK), 1)
    ).astype(BF)
    key = jnp.where(taken > 0.5, dot(taken.astype(BF), earlier), -10000.0)
    for h in range(2):
        meta[h, 0, 0:NEXP, :] = key
        meta[h, 0, NEXP : 2 * NEXP, :] = weight

    pl.semaphore_wait(barrier, len(peers))

    for h in range(2):
        for r in (1, 2, 3):
            remote(meta.at[h, 0], meta.at[h, 4 - r], ms.at[h], mr.at[h], spread[h](r)).start()

    neighbour = (4 - 1, 1)

    def gather_own(a, h, i):
        load(a, h, i).wait()
        buf = arrays[a][1].at[h, i]
        for k, r in ((0, 1), (1, 3)) if PASS else ((0, 1), (1, 3), (2, 2)):
            remote(
                buf.at[pl.ds(0, TOK)],
                buf.at[pl.ds((4 - r) * TOK, TOK)],
                ags.at[a, h, i],
                agr.at[a, h, i, k],
                spread[h](r),
            ).start()

    def gather_pass(a, h, i):
        buf = arrays[a][1].at[h, i]
        for k, r in ((0, 1), (1, 3)):
            part = buf.at[pl.ds(neighbour[k] * TOK, TOK)]
            remote(part, part, ags.at[a, h, i], agr.at[a, h, i, k], spread[h](r)).wait_recv()
            if not PASS:
                continue
            remote(
                buf.at[pl.ds(neighbour[k] * TOK + k * (TOK // 2), TOK // 2)],
                buf.at[pl.ds(2 * TOK + k * (TOK // 2), TOK // 2)],
                ags.at[a, h, i],
                agr.at[a, h, i, 2],
                spread[h](r),
            ).start()

    def gather_far(a, h, i):
        part = arrays[a][1].at[h, i, pl.ds(2 * TOK, TOK)]
        remote(part, part, ags.at[a, h, i], agr.at[a, h, i, 2], spread[h](1)).wait_recv()

    def gather_all(a, h, i):
        part = arrays[a][1].at[h, i, pl.ds(TOK, 3 * TOK)]
        return remote(part, part, ags.at[a, h, i], agr.at[a, h, i, 0], spread[h](1))

    for n in range(LOOK):
        for h in range(2):
            gather_own(n // 4, h, n % 4)

    for m, (src, dst) in enumerate(((wg_hbm, wg), (wu_hbm, wu), (wd_hbm, wd))):
        for h in range(2):
            for i in range(4):
                cols = pl.ds(pl.multiple_of(block(h, i) * FB, FB), FB)
                pltpu.make_async_copy(src.at[0, :, cols], dst.at[h, i], wsem.at[m, h, i]).start()

    for h in range(2):
        m = meta.at[h, pl.ds(1, 3)]
        remote(m, m, ms.at[h], mr.at[h], spread[h](1)).wait()
        for r in range(4):
            ex = route[h](r)[1]
            keys = jnp.concatenate([meta[h, s, pl.ds(ex, 1), :] + float(s * CAP) for s in range(4)], axis=1)
            wts = jnp.concatenate([meta[h, s, pl.ds(ex + NEXP, 1), :] for s in range(4)], axis=1)
            hit = lax.broadcasted_iota(jnp.int32, (ROWS, 4 * TOK), 0).astype(F32) == keys
            pmat[h, r * ROWS : (r + 1) * ROWS, :] = jnp.where(hit, 1.0, 0.0).astype(BF)
            crow[h, r * ROWS : (r + 1) * ROWS, :] = jnp.sum(jnp.where(hit, wts, 0.0), axis=1, keepdims=True)

    def second_send(a, h, i):
        snd, dst = ((tsend, xin), (ssend, sin))[a]
        for r in (2, 1, 3):
            remote(
                snd.at[h, i, pl.ds(r * ROWS, ROWS)],
                dst.at[h, i, pl.ds((4 - r) * ROWS, ROWS)],
                a2s.at[a, h, i],
                a2r.at[a, h, i],
                route[h](r),
            ).start()

    def second_all(a, h, i):
        snd, dst = ((tsend, xin), (ssend, sin))[a]
        return remote(
            snd.at[h, i, pl.ds(ROWS, 3 * ROWS)],
            dst.at[h, i, pl.ds(ROWS, 3 * ROWS)],
            a2s.at[a, h, i],
            a2r.at[a, h, i],
            route[h](1),
        )

    def picked(a, h, i):
        gather_far(a, h, i)
        rows = dot(pmat[h], arrays[a][1][h, i])
        rows = (rows * crow[h] if a else rows).astype(BF)
        snd, dst = ((tsend, xin), (ssend, sin))[a]
        dst[h, i, 0:ROWS, :] = rows[0:ROWS]
        snd[h, i] = rows
        second_send(a, h, i)

    def exchange(n):
        for h in range(2):
            if n < 8 - AHEAD:
                gather_pass((n + AHEAD) // 4, h, (n + AHEAD) % 4)
            if n >= 4:
                gather_all(0, h, n - 4).wait_send()
        for h in range(2):
            picked(n // 4, h, n % 4)
        for h in range(2):
            if n >= LAG:
                second_all((n - LAG) // 4, h, (n - LAG) % 4).wait_send()
            if n < 8 - LOOK:
                gather_own((n + LOOK) // 4, h, (n + LOOK) % 4)

    def same_order(buf, i):
        val = buf[1, i].astype(F32)
        pieces = [val[p * ROWS + q * CAP : p * ROWS + (q + 1) * CAP] for q in range(4) for p in range(4)]
        buf[1, i] = jnp.concatenate(pieces, axis=0).astype(BF)

    def arrived(a, i):
        for h in range(2):
            second_all(a, h, i).wait_recv()
        same_order((xin, sin)[a], i)

    def big(r):
        return pl.ds(pl.multiple_of(r * 352, 352), 352)

    def tile(r):
        return pl.ds(pl.multiple_of(r * 176, 176), 176)

    def project(w, src, at, blocks):
        total = None
        for i in blocks:
            for h in range(2):
                term = dot(w[h, i, at, :], src[h, i], NT)
                total = term if total is None else total + term
        return total

    def gates(i):
        arrived(0, i)

        @pl.loop(0, 2)
        def _(r):
            for acc, w in ((gate, wg), (upper, wu)):
                val = project(w, xin, big(r), (i,))
                acc[big(r), :] = acc[big(r), :] + val if i else val

    def gates_end():
        @pl.loop(0, 4)
        def _(r):
            g, u = gate[tile(r), :], upper[tile(r), :]
            s = jax.nn.sigmoid(g)
            active = g * s
            hidden[tile(r), :] = (active * u).astype(BF)
            gate[tile(r), :] = u * s * (1.0 + g * (1.0 - s))
            upper[tile(r), :] = active

    outs = (out_d, out_g, out_u)

    def partial(m, h, i):
        val = dot((hidden, ggt, gut)[m][...], (sin if m == 0 else xin)[h, i])
        low, high = val[:, 0:TOK], val[:, TOK : 2 * TOK]
        own = jnp.where(c == 0, low, high)
        if h == 1 and i == 0:
            last[m] = own
        else:
            mine[m, h] = own
        csend[m, h] = jnp.where(c == 0, high, low).astype(BF)
        remote(csend.at[m, h], crecv.at[m, h, i], cs.at[m, h, i], cr.at[m, h, i], other_core).start()

    def swapped(m, h, i):
        remote(csend.at[m, h], crecv.at[m, h, i], cs.at[m, h, i], cr.at[m, h, i], other_core).wait()

    def zcopy(m, h, i, rows=pl.ds(0, HID)):
        return remote(
            zsend.at[m, h, i % 2, rows],
            zrecv.at[m, h, i, rows],
            zs.at[m, h, i],
            zr.at[m, h, i],
            along_z(1 if h == 0 else -1),
        )

    halves = (pl.ds(0, 352), pl.ds(352, 352))

    def forward(m, i):
        if i == 0:
            swapped(m, 0, 0)
            val = (mine[m, 0] + crecv[m, 0, 0].astype(F32)).astype(BF)
            for h in range(2):
                zsend[m, h, 0, halves[h], :] = val[352 * h : 352 * h + 352]
                zcopy(m, h, 0, halves[h]).start()
            return
        for h in range(2):
            swapped(m, h, i)
            if i == 1:
                zcopy(m, h, 0, halves[h]).wait_recv()
                val = mine[m, h] + crecv[m, h, 1].astype(F32)
                got = zrecv[m, h, 0, halves[h], :].astype(F32)
                keep = val[352 * (1 - h) : 352 * (1 - h) + 352]
                zsend[m, h, 1, halves[h], :] = (val[352 * h : 352 * h + 352] + got).astype(BF)
                zsend[m, h, 1, halves[1 - h], :] = keep.astype(BF)
            else:
                zcopy(m, h, i - 1).wait_recv()
                if i == 2:
                    zcopy(m, h, 0, halves[h]).wait_send()
                else:
                    zcopy(m, h, i - 2).wait_send()
                val = mine[m, h] + crecv[m, h, i].astype(F32) + zrecv[m, h, i - 1].astype(F32)
                zsend[m, h, i % 2] = val.astype(BF)
            zcopy(m, h, i).start()

    def settle(m):
        for h in range(2):
            zcopy(m, h, 3).wait_recv()
            zcopy(m, h, 2).wait_send()
            zcopy(m, h, 3).wait_send()
        near = last[m] + crecv[m, 1, 0].astype(F32)
        last[m] = near + (zrecv[m, 0, 3].astype(F32) + zrecv[m, 1, 3].astype(F32))
        pltpu.make_async_copy(last.at[m], outs[m].at[0], osem.at[m]).start()

    def back_copy(h, i, r):
        return remote(
            tsend.at[h, i, pl.ds(r * ROWS, ROWS)],
            brecv.at[h, i, pl.ds((4 - r) * ROWS, ROWS)],
            bs.at[h, i],
            br.at[h, i],
            route[h](r),
        )

    def back_all(h, i):
        return remote(
            tsend.at[h, i, pl.ds(ROWS, 3 * ROWS)],
            brecv.at[h, i, pl.ds(ROWS, 3 * ROWS)],
            bs.at[h, i],
            br.at[h, i],
            route[h](1),
        )

    def back(h, i):
        val = dot(gg[...], wg[h, i]) + dot(gu[...], wu[h, i])
        if h == 1:
            pieces = [val[p * ROWS + q * CAP : p * ROWS + (q + 1) * CAP] for q in range(4) for p in range(4)]
            val = jnp.concatenate(pieces, axis=0)
        val = val.astype(BF)
        brecv[h, i, 0:ROWS, :] = val[0:ROWS]
        tsend[h, i] = val
        for r in (2, 1, 3):
            back_copy(h, i, r).start()

    def home_all(h, i):
        return remote(
            ssend.at[h, i, pl.ds(TOK, 3 * TOK)],
            tbuf.at[h, i, pl.ds(TOK, 3 * TOK)],
            ps.at[h, i],
            pr.at[h, i],
            spread[h](1),
        )

    def home(h, i):
        back_all(h, i).wait_recv()
        if i >= 4 - LAG:
            second_all(1, h, i).wait_send()
        val = dot(pback[h], brecv[h, i]).astype(BF)
        tbuf[h, i, 0:TOK, :] = val[0:TOK]
        ssend[h, i, 0 : 4 * TOK, :] = val
        for s in (1, 3, 2):
            remote(
                ssend.at[h, i, pl.ds(s * TOK, TOK)],
                tbuf.at[h, i, pl.ds((4 - s) * TOK, TOK)],
                ps.at[h, i],
                pr.at[h, i],
                spread[h](s),
            ).start()

    def finish(h, i):
        home_all(h, i).wait_recv()
        total = tbuf[h, i, 0:TOK, :].astype(F32)
        for s in range(1, 4):
            total = total + tbuf[h, i, s * TOK : (s + 1) * TOK, :].astype(F32)
        cols = pl.ds(pl.multiple_of(block(h, i) * FB, FB), FB)
        home_rows[h, i] = total.astype(BF)
        pltpu.make_async_copy(home_rows.at[h, i], out_tok.at[:, cols], lsem.at[0, h, i]).start()

    def both(f, *args):
        f(0, *args)
        f(1, *args)

    def partials(m, i):
        partial(m, 0, i)
        partial(m, 1, i)

    def zero(m):
        partial(m, 1, 0)
        swapped(m, 1, 0)

    def down(i):
        arrived(1, i)
        partials(0, i) if i else partial(0, 0, 0)
        total = project(wd, sin, slice(None), (i,))
        gh[...] = total if i == 0 else gh[...] + total
        forward(0, i)

    for n in range(AHEAD):
        for h in range(2):
            gather_pass(0, h, n)
    exchange(0)
    exchange(1)
    exchange(2)
    wait_weights(0)
    wait_weights(1)
    gates(0)
    exchange(3)
    gates(1)
    exchange(4)
    gates(2)
    exchange(5)
    gates(3)
    gates_end()
    wait_weights(2)
    down(0)
    exchange(6)
    down(1)
    exchange(7)
    for h in range(2):
        pback[h] = pmat[h].T
    down(2)
    arrived(1, 3)
    partials(0, 3)

    @pl.loop(0, 2)
    def _(r):
        v = gh[big(r), :] + project(wd, sin, big(r), (3,))
        ggt[big(r), :] = (v * gate[big(r), :]).astype(BF)
        gut[big(r), :] = (v * upper[big(r), :]).astype(BF)

    partial(1, 0, 0)
    partial(2, 0, 0)
    gg[...] = ggt[...].T
    gu[...] = gut[...].T
    forward(1, 0)
    forward(0, 3)
    forward(2, 0)
    both(back, 0)
    partials(1, 1)
    both(back, 1)
    forward(1, 1)
    partials(2, 1)
    both(back, 2)
    forward(2, 1)
    partials(1, 2)
    both(back, 3)
    zero(0)
    forward(1, 2)
    partials(2, 2)
    settle(0)
    both(home, 0)
    forward(2, 2)
    partials(1, 3)
    both(home, 1)
    forward(1, 3)
    partials(2, 3)
    both(home, 2)
    forward(2, 3)
    both(home, 3)
    zero(1)
    both(finish, 0)
    both(finish, 1)
    settle(1)
    zero(2)
    both(finish, 2)
    both(finish, 3)
    settle(2)

    for h in range(2):
        for i in range(4):
            gather_all(1, h, i).wait_send()
            back_all(h, i).wait_send()
            home_all(h, i).wait_send()
            pltpu.make_async_copy(home_rows.at[h, i], out_tok.at[:, pl.ds(0, FB)], lsem.at[0, h, i]).wait()
    for m in range(3):
        pltpu.make_async_copy(last.at[m], outs[m].at[0], osem.at[m]).wait()


def deliver(*refs):
    ins, outs, held, sems = refs[0:4], refs[4:8], refs[8:12], refs[12]
    copies = [pltpu.make_async_copy(ins[n], held[n], sems.at[0, n]) for n in range(4)]
    back = [pltpu.make_async_copy(held[n], outs[n], sems.at[1, n]) for n in range(4)]
    for copy in copies:
        copy.start()
    for n in range(4):
        copies[n].wait()
        back[n].start()
    for copy in back:
        copy.wait()


def local(tokens, grad_out, routes, combine, w_gate, w_up, w_down):
    vm = pl.BlockSpec(memory_space=pltpu.VMEM)
    hbm = pl.BlockSpec(memory_space=pl.ANY)
    grad = jax.ShapeDtypeStruct((1, HID, TOK), F32)
    shapes = (jax.ShapeDtypeStruct((TOK, WID), BF), grad, grad, grad)
    sem = pltpu.SemaphoreType.DMA
    V = pltpu.VMEM
    parts = pl.pallas_call(
        kernel,
        name="experts",
        out_shape=shapes,
        in_specs=[hbm, hbm, vm, vm, hbm, hbm, hbm],
        out_specs=(hbm, hbm, hbm, hbm),
        scratch_shapes=[
            V((2, 4, HID, FB), BF), V((2, 4, HID, FB), BF), V((2, 4, HID, FB), BF),
            V((2, 4, 2 * NEXP, 128), F32),
            V((2, ALL, 4 * TOK), BF), V((2, 4 * TOK, ALL), BF),
            V((2, ALL, 1), F32),
            V((2, 4, 4 * TOK, FB), BF), V((2, 4, 4 * TOK, FB), BF),
            V((2, 4, ALL, FB), BF), V((2, 4, ALL, FB), BF),
            V((2, 4, ALL, FB), BF), V((2, 4, ALL, FB), BF),
            V((HID, ALL), F32), V((HID, ALL), F32), V((HID, ALL), F32),
            V((HID, ALL), BF), V((HID, ALL), BF), V((HID, ALL), BF),
            V((ALL, HID), BF), V((ALL, HID), BF),
            V((3, 2, HID, TOK), F32), V((3, HID, TOK), F32),
            V((3, 2, HID, TOK), BF),
            V((3, 2, 4, HID, TOK), BF),
            V((3, 2, 2, HID, TOK), BF),
            V((3, 2, 4, HID, TOK), BF),
            V((2, 4, ALL, FB), BF),
            V((2, 4, TOK, FB), BF),
            sem((3, 2, 4)), sem((2, 2, 4)), sem((3,)), sem((2,)), sem((2,)),
            sem((2, 2, 4)), sem((2, 2, 4, 3)), sem((2, 2, 4)), sem((2, 2, 4)),
            sem((3, 2, 4)), sem((3, 2, 4)), sem((3, 2, 4)), sem((3, 2, 4)),
            sem((2, 4)), sem((2, 4)), sem((2, 4)), sem((2, 4)),
        ],
        compiler_params=pltpu.CompilerParams(
            collective_id=0, has_side_effects=True, vmem_limit_bytes=62 * 2**20
        ),
        cost_estimate=pl.CostEstimate(flops=15 * 10**9, bytes_accessed=12 * 10**6, transcendentals=450560),
    )(tokens, grad_out, routes.T, combine.T, *[w.transpose(0, 2, 1) for w in (w_gate, w_up, w_down)])
    grad_tokens, *grads = pl.pallas_call(
        deliver,
        name="deliver",
        out_shape=shapes,
        in_specs=[hbm] * 4,
        out_specs=(hbm,) * 4,
        scratch_shapes=[V(o.shape, o.dtype) for o in shapes] + [sem((2, 4))],
    )(*parts)
    return (grad_tokens, *[g.transpose(0, 2, 1) for g in grads])


def solution(mesh):
    rows = P(("dp", "expert"), None)
    weights = P("expert", None, None)
    grads = P("expert", "dp", None)
    return jax.shard_map(
        local,
        mesh=mesh,
        in_specs=(rows, rows, rows, rows, weights, weights, weights),
        out_specs=(rows, grads, grads, grads),
        check_vma=False,
    )
```

```python
import jax
import jax.numpy as jnp
from jax import lax
from jax.experimental import pallas as pl
from jax.experimental.pallas import tpu as pltpu
from jax.sharding import PartitionSpec as P

AHEAD = 3
LOOK, LAG, PASS = 6, 3, True
MESH = pl.DeviceIdType.MESH
BF = jnp.bfloat16
F32 = jnp.float32
TOK, WID, HID, CAP, NEXP = 128, 2048, 704, 40, 16
FB = 256
ROWS = 4 * CAP
ALL = 4 * ROWS
NN = (((1,), (0,)), ((), ()))
NT = (((1,), (1,)), ((), ()))
TN = (((0,), (0,)), ((), ()))


def dot(a, b, dims=NN):
    return lax.dot_general(a, b, dims, preferred_element_type=F32)


def kernel(
    tok_hbm, go_hbm, routes_ref, comb_ref, wg_hbm, wu_hbm, wd_hbm,
    out_tok, out_g, out_u, out_d,
    wg, wu, wd, meta, pmat, pback, crow, tbuf, gbuf, tsend, ssend, xin, sin,
    gate, upper, gh, hidden, ggt, gut, gg, gu, mine, last, csend, crecv, zsend, zrecv, brecv, home_rows,
    wsem, lsem, osem, ms, mr, ags, agr, a2s, a2r, cs, cr, zs, zr, bs, br, ps, pr,
):
    e = lax.axis_index("expert")
    d = lax.axis_index("dp")
    x, y, z, c = lax.rem(e, 4), e // 4, d // 2, lax.rem(d, 2)

    def along_y(r):
        return (d, lax.rem(y + r, 4) * 4 + x)

    def along_x(r):
        return (d, y * 4 + lax.rem(x + r, 4))

    def along_z(r):
        return (lax.rem(z + r + 8, 8) * 2 + c, e)

    other_core = (z * 2 + 1 - c, e)
    spread = (along_y, along_x)
    route = (along_x, along_y)

    def block(h, i):
        if h == 0:
            return lax.rem(z + 4 - i, 8)
        return lax.rem(z + 4 + i, 8) if i else z

    def remote(src, dst, ss, rs, dev):
        return pltpu.make_async_remote_copy(
            src_ref=src, dst_ref=dst, send_sem=ss, recv_sem=rs, device_id=dev, device_id_type=MESH
        )

    barrier = pltpu.get_barrier_semaphore()
    peers = [f(r) for f in (along_x, along_y) for r in (1, 2, 3)] + [along_z(1), along_z(-1), other_core]
    for dev in peers:
        pl.semaphore_signal(barrier, inc=1, device_id=dev, device_id_type=MESH)

    arrays = ((tok_hbm, tbuf), (go_hbm, gbuf))

    def load(a, h, i):
        cols = pl.ds(pl.multiple_of(block(h, i) * FB, FB), FB)
        return pltpu.make_async_copy(
            arrays[a][0].at[:, cols], arrays[a][1].at[h, i, pl.ds(0, TOK)], lsem.at[a, h, i]
        )

    for a in range(2):
        for i in range(4):
            for h in range(2):
                load(a, h, i).start()
    def wait_weights(m):
        src, dst = ((wg_hbm, wg), (wu_hbm, wu), (wd_hbm, wd))[m]
        for h in range(2):
            for i in range(4):
                pltpu.make_async_copy(src.at[0, :, pl.ds(0, FB)], dst.at[h, i], wsem.at[m, h, i]).wait()

    experts = lax.broadcasted_iota(jnp.int32, (NEXP, TOK), 0)
    taken = jnp.zeros((NEXP, TOK), F32)
    weight = jnp.zeros((NEXP, TOK), F32)
    for k in range(4):
        hit = routes_ref[k : k + 1, :] == experts
        taken = taken + jnp.where(hit, 1.0, 0.0)
        weight = weight + jnp.where(hit, comb_ref[k : k + 1, :], 0.0)
    earlier = (
        lax.broadcasted_iota(jnp.int32, (TOK, TOK), 0) < lax.broadcasted_iota(jnp.int32, (TOK, TOK), 1)
    ).astype(BF)
    key = jnp.where(taken > 0.5, dot(taken.astype(BF), earlier), -10000.0)
    for h in range(2):
        meta[h, 0, 0:NEXP, :] = key
        meta[h, 0, NEXP : 2 * NEXP, :] = weight

    pl.semaphore_wait(barrier, len(peers))

    for h in range(2):
        for r in (1, 2, 3):
            remote(meta.at[h, 0], meta.at[h, 4 - r], ms.at[h], mr.at[h], spread[h](r)).start()

    neighbour = (4 - 1, 1)

    def gather_own(a, h, i):
        load(a, h, i).wait()
        buf = arrays[a][1].at[h, i]
        for k, r in ((0, 1), (1, 3)) if PASS else ((0, 1), (1, 3), (2, 2)):
            remote(
                buf.at[pl.ds(0, TOK)],
                buf.at[pl.ds((4 - r) * TOK, TOK)],
                ags.at[a, h, i],
                agr.at[a, h, i, k],
                spread[h](r),
            ).start()

    def gather_pass(a, h, i):
        buf = arrays[a][1].at[h, i]
        for k, r in ((0, 1), (1, 3)):
            part = buf.at[pl.ds(neighbour[k] * TOK, TOK)]
            remote(part, part, ags.at[a, h, i], agr.at[a, h, i, k], spread[h](r)).wait_recv()
            if not PASS:
                continue
            remote(
                buf.at[pl.ds(neighbour[k] * TOK + k * (TOK // 2), TOK // 2)],
                buf.at[pl.ds(2 * TOK + k * (TOK // 2), TOK // 2)],
                ags.at[a, h, i],
                agr.at[a, h, i, 2],
                spread[h](r),
            ).start()

    def gather_far(a, h, i):
        part = arrays[a][1].at[h, i, pl.ds(2 * TOK, TOK)]
        remote(part, part, ags.at[a, h, i], agr.at[a, h, i, 2], spread[h](1)).wait_recv()

    def gather_all(a, h, i):
        part = arrays[a][1].at[h, i, pl.ds(TOK, 3 * TOK)]
        return remote(part, part, ags.at[a, h, i], agr.at[a, h, i, 0], spread[h](1))

    for n in range(LOOK):
        for h in range(2):
            gather_own(n // 4, h, n % 4)

    for m, (src, dst) in enumerate(((wg_hbm, wg), (wu_hbm, wu), (wd_hbm, wd))):
        for h in range(2):
            for i in range(4):
                cols = pl.ds(pl.multiple_of(block(h, i) * FB, FB), FB)
                pltpu.make_async_copy(src.at[0, :, cols], dst.at[h, i], wsem.at[m, h, i]).start()

    for h in range(2):
        m = meta.at[h, pl.ds(1, 3)]
        remote(m, m, ms.at[h], mr.at[h], spread[h](1)).wait()
        for r in range(4):
            ex = route[h](r)[1]
            keys = jnp.concatenate([meta[h, s, pl.ds(ex, 1), :] + float(s * CAP) for s in range(4)], axis=1)
            wts = jnp.concatenate([meta[h, s, pl.ds(ex + NEXP, 1), :] for s in range(4)], axis=1)
            hit = lax.broadcasted_iota(jnp.int32, (ROWS, 4 * TOK), 0).astype(F32) == keys
            pmat[h, r * ROWS : (r + 1) * ROWS, :] = jnp.where(hit, 1.0, 0.0).astype(BF)
            crow[h, r * ROWS : (r + 1) * ROWS, :] = jnp.sum(jnp.where(hit, wts, 0.0), axis=1, keepdims=True)

    def second_send(a, h, i):
        snd, dst = ((tsend, xin), (ssend, sin))[a]
        for r in (2, 1, 3):
            remote(
                snd.at[h, i, pl.ds(r * ROWS, ROWS)],
                dst.at[h, i, pl.ds((4 - r) * ROWS, ROWS)],
                a2s.at[a, h, i],
                a2r.at[a, h, i],
                route[h](r),
            ).start()

    def second_all(a, h, i):
        snd, dst = ((tsend, xin), (ssend, sin))[a]
        return remote(
            snd.at[h, i, pl.ds(ROWS, 3 * ROWS)],
            dst.at[h, i, pl.ds(ROWS, 3 * ROWS)],
            a2s.at[a, h, i],
            a2r.at[a, h, i],
            route[h](1),
        )

    def picked(a, h, i):
        gather_far(a, h, i)
        rows = dot(pmat[h], arrays[a][1][h, i])
        rows = (rows * crow[h] if a else rows).astype(BF)
        snd, dst = ((tsend, xin), (ssend, sin))[a]
        dst[h, i, 0:ROWS, :] = rows[0:ROWS]
        snd[h, i] = rows
        second_send(a, h, i)

    def exchange(n):
        for h in range(2):
            if n < 8 - AHEAD:
                gather_pass((n + AHEAD) // 4, h, (n + AHEAD) % 4)
            if n >= 4:
                gather_all(0, h, n - 4).wait_send()
        for h in range(2):
            picked(n // 4, h, n % 4)
        for h in range(2):
            if n >= LAG:
                second_all((n - LAG) // 4, h, (n - LAG) % 4).wait_send()
            if n < 8 - LOOK:
                gather_own((n + LOOK) // 4, h, (n + LOOK) % 4)

    def same_order(buf, i):
        val = buf[1, i].astype(F32)
        pieces = [val[p * ROWS + q * CAP : p * ROWS + (q + 1) * CAP] for q in range(4) for p in range(4)]
        buf[1, i] = jnp.concatenate(pieces, axis=0).astype(BF)

    def arrived(a, i):
        for h in range(2):
            second_all(a, h, i).wait_recv()
        same_order((xin, sin)[a], i)

    def big(r):
        return pl.ds(pl.multiple_of(r * 352, 352), 352)

    def tile(r):
        return pl.ds(pl.multiple_of(r * 176, 176), 176)

    def project(w, src, at, blocks):
        total = None
        for i in blocks:
            for h in range(2):
                term = dot(w[h, i, at, :], src[h, i], NT)
                total = term if total is None else total + term
        return total

    def gates(i):
        arrived(0, i)

        @pl.loop(0, 2)
        def _(r):
            for acc, w in ((gate, wg), (upper, wu)):
                val = project(w, xin, big(r), (i,))
                acc[big(r), :] = acc[big(r), :] + val if i else val

    def gates_end():
        @pl.loop(0, 4)
        def _(r):
            g, u = gate[tile(r), :], upper[tile(r), :]
            s = jax.nn.sigmoid(g)
            active = g * s
            hidden[tile(r), :] = (active * u).astype(BF)
            gate[tile(r), :] = u * s * (1.0 + g * (1.0 - s))
            upper[tile(r), :] = active

    outs = (out_d, out_g, out_u)

    def partial(m, h, i):
        val = dot((hidden, ggt, gut)[m][...], (sin if m == 0 else xin)[h, i])
        low, high = val[:, 0:TOK], val[:, TOK : 2 * TOK]
        own = jnp.where(c == 0, low, high)
        if h == 1 and i == 0:
            last[m] = own
        else:
            mine[m, h] = own
        csend[m, h] = jnp.where(c == 0, high, low).astype(BF)
        remote(csend.at[m, h], crecv.at[m, h, i], cs.at[m, h, i], cr.at[m, h, i], other_core).start()

    def swapped(m, h, i):
        remote(csend.at[m, h], crecv.at[m, h, i], cs.at[m, h, i], cr.at[m, h, i], other_core).wait()

    def zcopy(m, h, i, rows=pl.ds(0, HID)):
        return remote(
            zsend.at[m, h, i % 2, rows],
            zrecv.at[m, h, i, rows],
            zs.at[m, h, i],
            zr.at[m, h, i],
            along_z(1 if h == 0 else -1),
        )

    halves = (pl.ds(0, 352), pl.ds(352, 352))

    def forward(m, i):
        if i == 0:
            swapped(m, 0, 0)
            val = (mine[m, 0] + crecv[m, 0, 0].astype(F32)).astype(BF)
            for h in range(2):
                zsend[m, h, 0, halves[h], :] = val[352 * h : 352 * h + 352]
                zcopy(m, h, 0, halves[h]).start()
            return
        for h in range(2):
            swapped(m, h, i)
            if i == 1:
                zcopy(m, h, 0, halves[h]).wait_recv()
                val = mine[m, h] + crecv[m, h, 1].astype(F32)
                got = zrecv[m, h, 0, halves[h], :].astype(F32)
                keep = val[352 * (1 - h) : 352 * (1 - h) + 352]
                zsend[m, h, 1, halves[h], :] = (val[352 * h : 352 * h + 352] + got).astype(BF)
                zsend[m, h, 1, halves[1 - h], :] = keep.astype(BF)
            else:
                zcopy(m, h, i - 1).wait_recv()
                if i == 2:
                    zcopy(m, h, 0, halves[h]).wait_send()
                else:
                    zcopy(m, h, i - 2).wait_send()
                val = mine[m, h] + crecv[m, h, i].astype(F32) + zrecv[m, h, i - 1].astype(F32)
                zsend[m, h, i % 2] = val.astype(BF)
            zcopy(m, h, i).start()

    def settle(m):
        for h in range(2):
            zcopy(m, h, 3).wait_recv()
            zcopy(m, h, 2).wait_send()
            zcopy(m, h, 3).wait_send()
        near = last[m] + crecv[m, 1, 0].astype(F32)
        last[m] = near + (zrecv[m, 0, 3].astype(F32) + zrecv[m, 1, 3].astype(F32))
        pltpu.make_async_copy(last.at[m], outs[m].at[0], osem.at[m]).start()

    def back_copy(h, i, r):
        return remote(
            tsend.at[h, i, pl.ds(r * ROWS, ROWS)],
            brecv.at[h, i, pl.ds((4 - r) * ROWS, ROWS)],
            bs.at[h, i],
            br.at[h, i],
            route[h](r),
        )

    def back_all(h, i):
        return remote(
            tsend.at[h, i, pl.ds(ROWS, 3 * ROWS)],
            brecv.at[h, i, pl.ds(ROWS, 3 * ROWS)],
            bs.at[h, i],
            br.at[h, i],
            route[h](1),
        )

    def back(h, i):
        val = dot(gg[...], wg[h, i]) + dot(gu[...], wu[h, i])
        if h == 1:
            pieces = [val[p * ROWS + q * CAP : p * ROWS + (q + 1) * CAP] for q in range(4) for p in range(4)]
            val = jnp.concatenate(pieces, axis=0)
        val = val.astype(BF)
        brecv[h, i, 0:ROWS, :] = val[0:ROWS]
        tsend[h, i] = val
        for r in (2, 1, 3):
            back_copy(h, i, r).start()

    def home_all(h, i):
        return remote(
            ssend.at[h, i, pl.ds(TOK, 3 * TOK)],
            tbuf.at[h, i, pl.ds(TOK, 3 * TOK)],
            ps.at[h, i],
            pr.at[h, i],
            spread[h](1),
        )

    def home(h, i):
        back_all(h, i).wait_recv()
        if i >= 4 - LAG:
            second_all(1, h, i).wait_send()
        val = dot(pback[h], brecv[h, i]).astype(BF)
        tbuf[h, i, 0:TOK, :] = val[0:TOK]
        ssend[h, i, 0 : 4 * TOK, :] = val
        for s in (1, 3, 2):
            remote(
                ssend.at[h, i, pl.ds(s * TOK, TOK)],
                tbuf.at[h, i, pl.ds((4 - s) * TOK, TOK)],
                ps.at[h, i],
                pr.at[h, i],
                spread[h](s),
            ).start()

    def finish(h, i):
        home_all(h, i).wait_recv()
        total = tbuf[h, i, 0:TOK, :].astype(F32)
        for s in range(1, 4):
            total = total + tbuf[h, i, s * TOK : (s + 1) * TOK, :].astype(F32)
        cols = pl.ds(pl.multiple_of(block(h, i) * FB, FB), FB)
        home_rows[h, i] = total.astype(BF)
        pltpu.make_async_copy(home_rows.at[h, i], out_tok.at[:, cols], lsem.at[0, h, i]).start()

    def both(f, *args):
        f(0, *args)
        f(1, *args)

    def partials(m, i):
        partial(m, 0, i)
        partial(m, 1, i)

    def zero(m):
        partial(m, 1, 0)
        swapped(m, 1, 0)

    def down(i):
        arrived(1, i)
        partials(0, i) if i else partial(0, 0, 0)
        total = project(wd, sin, slice(None), (i,))
        gh[...] = total if i == 0 else gh[...] + total
        forward(0, i)

    for n in range(AHEAD):
        for h in range(2):
            gather_pass(0, h, n)
    exchange(0)
    exchange(1)
    exchange(2)
    wait_weights(0)
    wait_weights(1)
    gates(0)
    exchange(3)
    gates(1)
    exchange(4)
    gates(2)
    exchange(5)
    gates(3)
    gates_end()
    wait_weights(2)
    down(0)
    exchange(6)
    down(1)
    exchange(7)
    for h in range(2):
        pback[h] = pmat[h].T
    down(2)
    arrived(1, 3)

    @pl.loop(0, 2)
    def _(r):
        v = gh[big(r), :] + project(wd, sin, big(r), (3,))
        ggt[big(r), :] = (v * gate[big(r), :]).astype(BF)
        gut[big(r), :] = (v * upper[big(r), :]).astype(BF)

    partial(1, 0, 0)
    partial(2, 0, 0)
    partials(0, 3)
    gg[...] = ggt[...].T
    gu[...] = gut[...].T
    forward(1, 0)
    forward(0, 3)
    forward(2, 0)
    both(back, 0)
    partials(1, 1)
    both(back, 1)
    forward(1, 1)
    partials(2, 1)
    both(back, 2)
    forward(2, 1)
    partials(1, 2)
    both(back, 3)
    zero(0)
    forward(1, 2)
    partials(2, 2)
    settle(0)
    both(home, 0)
    forward(2, 2)
    partials(1, 3)
    both(home, 1)
    forward(1, 3)
    partials(2, 3)
    both(home, 2)
    forward(2, 3)
    both(home, 3)
    zero(1)
    both(finish, 0)
    both(finish, 1)
    settle(1)
    zero(2)
    both(finish, 2)
    both(finish, 3)
    settle(2)

    for h in range(2):
        for i in range(4):
            gather_all(1, h, i).wait_send()
            back_all(h, i).wait_send()
            home_all(h, i).wait_send()
            pltpu.make_async_copy(home_rows.at[h, i], out_tok.at[:, pl.ds(0, FB)], lsem.at[0, h, i]).wait()
    for m in range(3):
        pltpu.make_async_copy(last.at[m], outs[m].at[0], osem.at[m]).wait()


def deliver(*refs):
    ins, outs, held, sems = refs[0:4], refs[4:8], refs[8:12], refs[12]
    copies = [pltpu.make_async_copy(ins[n], held[n], sems.at[0, n]) for n in range(4)]
    back = [pltpu.make_async_copy(held[n], outs[n], sems.at[1, n]) for n in range(4)]
    for copy in copies:
        copy.start()
    for n in range(4):
        copies[n].wait()
        back[n].start()
    for copy in back:
        copy.wait()


def local(tokens, grad_out, routes, combine, w_gate, w_up, w_down):
    vm = pl.BlockSpec(memory_space=pltpu.VMEM)
    hbm = pl.BlockSpec(memory_space=pl.ANY)
    grad = jax.ShapeDtypeStruct((1, HID, TOK), F32)
    shapes = (jax.ShapeDtypeStruct((TOK, WID), BF), grad, grad, grad)
    sem = pltpu.SemaphoreType.DMA
    V = pltpu.VMEM
    parts = pl.pallas_call(
        kernel,
        name="experts",
        out_shape=shapes,
        in_specs=[hbm, hbm, vm, vm, hbm, hbm, hbm],
        out_specs=(hbm, hbm, hbm, hbm),
        scratch_shapes=[
            V((2, 4, HID, FB), BF), V((2, 4, HID, FB), BF), V((2, 4, HID, FB), BF),
            V((2, 4, 2 * NEXP, 128), F32),
            V((2, ALL, 4 * TOK), BF), V((2, 4 * TOK, ALL), BF),
            V((2, ALL, 1), F32),
            V((2, 4, 4 * TOK, FB), BF), V((2, 4, 4 * TOK, FB), BF),
            V((2, 4, ALL, FB), BF), V((2, 4, ALL, FB), BF),
            V((2, 4, ALL, FB), BF), V((2, 4, ALL, FB), BF),
            V((HID, ALL), F32), V((HID, ALL), F32), V((HID, ALL), F32),
            V((HID, ALL), BF), V((HID, ALL), BF), V((HID, ALL), BF),
            V((ALL, HID), BF), V((ALL, HID), BF),
            V((3, 2, HID, TOK), F32), V((3, HID, TOK), F32),
            V((3, 2, HID, TOK), BF),
            V((3, 2, 4, HID, TOK), BF),
            V((3, 2, 2, HID, TOK), BF),
            V((3, 2, 4, HID, TOK), BF),
            V((2, 4, ALL, FB), BF),
            V((2, 4, TOK, FB), BF),
            sem((3, 2, 4)), sem((2, 2, 4)), sem((3,)), sem((2,)), sem((2,)),
            sem((2, 2, 4)), sem((2, 2, 4, 3)), sem((2, 2, 4)), sem((2, 2, 4)),
            sem((3, 2, 4)), sem((3, 2, 4)), sem((3, 2, 4)), sem((3, 2, 4)),
            sem((2, 4)), sem((2, 4)), sem((2, 4)), sem((2, 4)),
        ],
        compiler_params=pltpu.CompilerParams(
            collective_id=0, has_side_effects=True, vmem_limit_bytes=62 * 2**20
        ),
        cost_estimate=pl.CostEstimate(flops=15 * 10**9, bytes_accessed=12 * 10**6, transcendentals=450560),
    )(tokens, grad_out, routes.T, combine.T, *[w.transpose(0, 2, 1) for w in (w_gate, w_up, w_down)])
    grad_tokens, *grads = pl.pallas_call(
        deliver,
        name="deliver",
        out_shape=shapes,
        in_specs=[hbm] * 4,
        out_specs=(hbm,) * 4,
        scratch_shapes=[V(o.shape, o.dtype) for o in shapes] + [sem((2, 4))],
    )(*parts)
    return (grad_tokens, *[g.transpose(0, 2, 1) for g in grads])


def solution(mesh):
    rows = P(("dp", "expert"), None)
    weights = P("expert", None, None)
    grads = P("expert", "dp", None)
    return jax.shard_map(
        local,
        mesh=mesh,
        in_specs=(rows, rows, rows, rows, weights, weights, weights),
        out_specs=(rows, grads, grads, grads),
        check_vma=False,
    )
```
